32 devices in a mesh: grp: 4 (over x, core), dev: 8 (over z, y).
Axes of the slice: x: 2, y: 2, z: 4, core: 2. Of those that a mesh axis runs over, the one named last changes fastest.
Arguments:
- traces: float32 [32, 16, 128], P(('grp', 'dev')), parts along dimension 0
- half_window: int32 [32], P(('grp', 'dev')), parts along dimension 0, may hold values from 4 to 23
- dip_slopes: int32 [9], replicated, may hold values from -4 to 4, as said below
Outputs:
- coherence: float32 [32, 16, 128], P('grp', 'dev'), parts along dimension 0
The draws below stay inside these ranges and needn't reach their ends.
There are 4 independent parts, one for each index of `grp`. The reference program is written for one: setup_inputs(seed, part) draws one part's arguments, and reference() takes and returns one part's arrays. A program takes and returns all parts, laid end to end along the dimension named above; an argument that names none is the same for every part. Nothing has to cross between parts.
Inputs may be any that keep to these rules, and one draw needn't show every extreme that they name: `dip_slopes`: each trial dip is a whole number of samples per shot; both extreme dips occur.
All inputs are finite; a program needn't handle non-finite values.
Results may differ from the reference program's by a relative error of at most 0.00005.
Values sent between devices are 32-bit elements; how exact they have to be, the bound alone decides.
A program may use at most 64 MiB of HBM per device.

```python
import jax
import jax.numpy as jnp
from jax import lax

NT = 128
NDIP = 9
MAXDIP = 4
SHOTS = 8
RECV = 16


def draw_traces(key, part):
    noise_key = jax.random.fold_in(key, 11)
    level_key = jax.random.fold_in(key, 12)
    noise = jax.random.normal(noise_key, (SHOTS, RECV, NT), jnp.float32)
    levels = jax.random.uniform(level_key, (SHOTS, RECV, NT // 16), jnp.float32, -3.0, 1.6)
    envelope = jnp.repeat(jnp.exp(levels), 16, axis=2)
    return (noise * envelope).astype(jnp.float32)


def draw_dip_slopes(key, part):
    chosen = jax.random.randint(jax.random.fold_in(key, 21), (NDIP,), -MAXDIP, MAXDIP + 1, jnp.int32)
    order = jax.random.permutation(jax.random.fold_in(key, 22), NDIP)
    chosen = chosen.at[order[0]].set(MAXDIP)
    chosen = chosen.at[order[1]].set(-MAXDIP)
    return chosen.astype(jnp.int32)


def place_ends(entries, rng, smallest, high):
    shape = entries.shape
    spot = [jax.random.randint(jax.random.fold_in(rng, axis), (), 0, shape[axis]) for axis in range(len(shape))]
    entries = entries.at[tuple(spot)].set(smallest)
    longest = shape.index(max(shape))
    spot[longest] = (spot[longest] + 1) % shape[longest]
    return entries.at[tuple(spot)].set(high)


def setup_inputs(seed: int = 0, part: int = 0) -> dict:
    key_list = jax.random.split(jax.random.key(seed), 4)
    part_keys = jax.random.split(jax.random.fold_in(key_list[3], part), 4)
    traces = draw_traces(jax.random.fold_in(jax.random.fold_in(key_list[3], part), 71), part)
    half_window = place_ends(jax.random.randint(part_keys[1], (SHOTS,), 4, 24), jax.random.fold_in(part_keys[1], 1), 4, 23).astype(jnp.int32)
    dip_slopes = draw_dip_slopes(jax.random.fold_in(key_list[3], 71), part)
    return {"traces": traces, "half_window": half_window, "dip_slopes": dip_slopes}


floor_level = 0.05

def gain_control(traces, half_window):
    samples = jnp.arange(traces.shape[-1], dtype=jnp.int32)
    distance = jnp.abs(samples[:, None] - samples[None, :])
    window_mask = (distance[None, :, :] <= half_window[:, None, None]).astype(jnp.float32)
    window_count = lax.optimization_barrier(jnp.sum(window_mask, axis=1))
    power_sum = jnp.einsum('srt,stu->sru', traces * traces, window_mask, precision=lax.Precision.HIGHEST)
    mean_square = power_sum / window_count[:, None, :]
    return traces * lax.rsqrt(jnp.maximum(mean_square, floor_level))

def semblance_scan(widened, dip_slopes):
    shot_count = widened.shape[0]
    wide = widened.shape[1]
    length = widened.shape[2]
    inner = wide - 4
    padded = jnp.pad(widened, ((2, 2), (0, 0), (13, 13)))
    coherent = None
    for which in range(dip_slopes.shape[0]):
        slope = dip_slopes[which].astype(jnp.int32)
        stacked = jnp.zeros((shot_count, wide, length + 10), jnp.float32)
        energy_sum = jnp.zeros((shot_count, wide, length + 10), jnp.float32)
        for member in range(5):
            offset = member - 2
            rows = padded[member:member + shot_count, :, :]
            start = (8 + offset * slope).astype(jnp.int32)
            shifted = lax.dynamic_slice_in_dim(rows, start, length + 10, 2)
            stacked = stacked + shifted
            energy_sum = energy_sum + shifted * shifted
        squared = stacked * stacked
        squared_rows = jnp.zeros((shot_count, inner, length + 10), jnp.float32)
        energy_rows = jnp.zeros((shot_count, inner, length + 10), jnp.float32)
        for across in range(5):
            squared_rows = squared_rows + squared[:, across:across + inner, :]
            energy_rows = energy_rows + energy_sum[:, across:across + inner, :]
        numerator = jnp.zeros((shot_count, inner, length), jnp.float32)
        denominator = jnp.zeros((shot_count, inner, length), jnp.float32)
        for lag in range(11):
            numerator = numerator + squared_rows[:, :, lag:lag + length]
            denominator = denominator + energy_rows[:, :, lag:lag + length]
        current = numerator / (5.0 * denominator + 1.0)
        coherent = current if coherent is None else jnp.maximum(coherent, current)
    return coherent

def reference(traces, half_window, dip_slopes):
    balanced = gain_control(traces, half_window)
    widened = jnp.pad(balanced, ((0, 0), (2, 2), (0, 0)))
    return semblance_scan(widened, dip_slopes)
```

```python
import functools

import jax
import jax.numpy as jnp
from jax import lax
from jax.experimental import pallas as pl
from jax.experimental.pallas import tpu as pltpu
from jax.sharding import PartitionSpec as P

MESH = pl.DeviceIdType.MESH
FLOOR = 0.05
HALF_RECV = 2
HALF_TIME = 5
MAXDIP = 4
TILE = 8


def ahead(value, amount):
    length = value.shape[-1]
    shift = (-amount) % length
    return value if shift == 0 else pltpu.roll(value, shift, value.ndim - 1)


def box(value):
    two = value + ahead(value, 1)
    four = two + ahead(two, 2)
    eight = four + ahead(four, 4)
    return (eight + ahead(two, 8)) + ahead(value, 10)


def recv_sums(rows, inner):
    if inner == 2:
        common = (rows[1] + rows[2]) + (rows[3] + rows[4])
        return [common + rows[0], common + rows[5]]
    return [functools.reduce(jnp.add, rows[o : o + 5]) for o in range(inner)]


def kernel(
    n, shots, recv, inner, rp,
    traces_ref, window_ref, dips_ref, out_ref,
    pad, send, buf, boxed, send_sem, recv_sem,
):
    length = traces_ref.shape[-1]
    me = lax.axis_index("dev")
    unroll = n <= 16

    def each(low, high, body):
        if unroll:
            for i in range(low, high):
                body(i)
        else:
            lax.fori_loop(low, high, lambda i, c: (body(i), c)[1], 0)

    barrier = pltpu.get_barrier_semaphore()

    def greet(d):
        pl.semaphore_signal(
            barrier, inc=1, device_id={"dev": lax.rem(me + d, n)}, device_id_type=MESH
        )

    each(1, n, greet)

    half = window_ref[0]
    values = traces_ref[0]
    later = lax.broadcasted_iota(jnp.int32, (length, length), 0)
    earlier = lax.broadcasted_iota(jnp.int32, (length, length), 1)
    near = (jnp.abs(later - earlier) <= half).astype(jnp.float32)
    power = jnp.dot(
        values * values, near,
        precision=lax.Precision.HIGHEST, preferred_element_type=jnp.float32,
    )
    sample = lax.broadcasted_iota(jnp.int32, (1, length), 1)
    count = jnp.minimum(sample + half, length - 1) - jnp.maximum(sample - half, 0) + 1
    balanced = values * lax.rsqrt(jnp.maximum(power / count.astype(jnp.float32), FLOOR))
    pad[0:HALF_RECV, :] = jnp.zeros((HALF_RECV, length), jnp.float32)
    pad[HALF_RECV : HALF_RECV + recv, :] = balanced
    tail = pad.shape[0] - HALF_RECV - recv
    pad[HALF_RECV + recv :, :] = jnp.zeros((tail, length), jnp.float32)

    def pack(d):
        send[d] = pad[pl.ds(d * inner, rp), :]

    each(0, n, pack)
    edge = jnp.zeros((2 * rp, length), jnp.float32)
    buf[0 : 2 * rp, :] = edge
    buf[(shots + 2) * rp :, :] = edge
    for ref in range(2 * inner):
        boxed[ref, 0:TILE, :] = jnp.zeros((TILE, length), jnp.float32)
        boxed[ref, TILE + shots :, :] = jnp.zeros((TILE, length), jnp.float32)
    weights = []
    for dip in range(-MAXDIP, MAXDIP + 1):
        found = dips_ref[0] == dip
        for i in range(1, dips_ref.shape[0]):
            found = jnp.logical_or(found, dips_ref[i] == dip)
        weights.append(jnp.where(found, 1.0, 0.0).astype(jnp.float32))

    pl.semaphore_wait(barrier, n - 1)

    def block(shot):
        return buf.at[pl.ds(pl.multiple_of((shot + 2) * rp, TILE), rp), :]

    def outgoing(d):
        peer = lax.rem(me + d, n)
        return pltpu.make_async_remote_copy(
            src_ref=send.at[peer],
            dst_ref=block(me),
            send_sem=send_sem.at[d],
            recv_sem=recv_sem.at[d],
            device_id={"dev": peer},
            device_id_type=MESH,
        )

    each(1, n, lambda d: outgoing(d).start())
    buf[pl.ds(pl.multiple_of((me + 2) * rp, TILE), rp), :] = send[me]

    def arrived(d):
        source = lax.rem(me + n - d, n)
        pltpu.make_async_remote_copy(
            src_ref=send.at[source],
            dst_ref=block(source),
            send_sem=send_sem.at[d],
            recv_sem=recv_sem.at[d],
            device_id={"dev": source},
            device_id_type=MESH,
        ).wait_recv()

    each(1, n, arrived)

    lane = lax.broadcasted_iota(jnp.int32, (TILE, length), 1)
    sides = (lane < 3 * length // 4, lane >= length // 4)

    def member(first, r, k):
        start = (first + k + 2) * rp + r
        return buf[pl.ds(start, TILE, stride=rp), :]

    def energies(first):
        squares = []
        for r in range(inner + 4):
            own = member(first, r, 0)
            squares.append(own * own)
        for o, total in enumerate(recv_sums(squares, inner)):
            for side in range(2):
                boxed[2 * o + side, pl.ds(first + TILE, TILE), :] = box(
                    jnp.where(sides[side], total, 0.0)
                )

    def scan(first):
        best = [[None, None] for _ in range(inner)]
        for dip in range(-MAXDIP, MAXDIP + 1):
            for side in range(2):
                squares = []
                for r in range(inner + 4):
                    terms = [
                        ahead(jnp.where(sides[side], member(first, r, k), 0.0), k * dip)
                        for k in range(-2, 3)
                    ]
                    total = ((terms[0] + terms[1]) + (terms[3] + terms[4])) + terms[2]
                    squares.append(total * total)
                for o, total in enumerate(recv_sums(squares, inner)):
                    terms = [
                        ahead(boxed[2 * o + side, pl.ds(first + TILE + k, TILE), :], k * dip)
                        for k in range(-2, 3)
                    ]
                    energy = ((terms[0] + terms[1]) + (terms[3] + terms[4])) + terms[2]
                    current = box(total) * weights[dip + MAXDIP] / (5.0 * energy + 1.0)
                    held = best[o][side]
                    best[o][side] = current if held is None else jnp.maximum(held, current)
        for o in range(inner):
            low, high = (ahead(best[o][side], -HALF_TIME) for side in range(2))
            out_ref[o, pl.ds(first, TILE), :] = jnp.where(lane < length // 2, low, high)

    blocks = shots // TILE
    if blocks == 1:
        energies(0)
        scan(0)
    else:
        lax.fori_loop(0, blocks, lambda i, c: (energies(pl.multiple_of(i * TILE, TILE)), c)[1], 0)
        lax.fori_loop(0, blocks, lambda i, c: (scan(pl.multiple_of(i * TILE, TILE)), c)[1], 0)

    each(1, n, lambda d: outgoing(d).wait_send())


def body(n, traces, half_window, dip_slopes):
    _, recv, length = traces.shape
    shots = n
    inner = recv // n
    rp = -(-(inner + 2 * HALF_RECV) // TILE) * TILE
    result = pl.pallas_call(
        functools.partial(kernel, n, shots, recv, inner, rp),
        out_shape=jax.ShapeDtypeStruct((inner, shots, length), jnp.float32),
        in_specs=[
            pl.BlockSpec(memory_space=pltpu.VMEM),
            pl.BlockSpec(memory_space=pltpu.SMEM),
            pl.BlockSpec(memory_space=pltpu.SMEM),
        ],
        out_specs=pl.BlockSpec(memory_space=pltpu.VMEM),
        scratch_shapes=[
            pltpu.VMEM((recv + rp, length), jnp.float32),
            pltpu.VMEM((n, rp, length), jnp.float32),
            pltpu.VMEM(((shots + 4) * rp, length), jnp.float32),
            pltpu.VMEM((2 * inner, shots + 2 * TILE, length), jnp.float32),
            pltpu.SemaphoreType.DMA((n,)),
            pltpu.SemaphoreType.DMA((n,)),
        ],
        compiler_params=pltpu.CompilerParams(
            collective_id=0, has_side_effects=True, vmem_limit_bytes=24 * 1024 * 1024
        ),
    )(traces, half_window, dip_slopes)
    return jnp.swapaxes(result, 0, 1)


def solution(mesh):
    return jax.shard_map(
        functools.partial(body, mesh.shape["dev"]),
        mesh=mesh,
        in_specs=(P(("grp", "dev"), None, None), P(("grp", "dev")), P()),
        out_specs=P("grp", "dev", None),
        check_vma=False,
    )
```

```python
import functools

import jax
import jax.numpy as jnp
from jax import lax
from jax.experimental import pallas as pl
from jax.experimental.pallas import tpu as pltpu
from jax.sharding import PartitionSpec as P

MESH = pl.DeviceIdType.MESH
FLOOR = 0.05
HALF_RECV = 2
HALF_TIME = 5
MAXDIP = 4
TILE = 8


def ahead(value, amount):
    length = value.shape[-1]
    shift = (length - amount) % length if isinstance(amount, int) else lax.rem(length - amount, length)
    return value if isinstance(amount, int) and amount == 0 else pltpu.roll(value, shift, value.ndim - 1)


def centred_box(value):
    three = (ahead(value, -1) + ahead(value, 1)) + value
    nine = (ahead(three, -3) + ahead(three, 3)) + three
    return nine + (ahead(value, -5) + ahead(value, 5))


def recv_sums(rows, inner):
    if inner == 2:
        common = (rows[1] + rows[2]) + (rows[3] + rows[4])
        return [common + rows[0], common + rows[5]]
    return [functools.reduce(jnp.add, rows[o : o + 5]) for o in range(inner)]


def kernel(
    n, shots, recv, inner, rp,
    traces_hbm, window_hbm, dips_hbm, out_ref,
    traces_ref, window_ref, dips_ref, load_sem,    pad, send, buf, line, summed, band, weight, send_sem, recv_sem,
):
    length = traces_hbm.shape[-1]
    me = lax.axis_index("dev")
    unroll = n <= 16
    wide = inner + 4
    shifts = sorted({k * dip for k in range(3) for dip in range(-MAXDIP, MAXDIP + 1)})

    def each(low, high, body):
        if unroll:
            for i in range(low, high):
                body(i)
        else:
            lax.fori_loop(low, high, lambda i, c: (body(i), c)[1], 0)

    barrier = pltpu.get_barrier_semaphore()

    def greet(d):
        pl.semaphore_signal(
            barrier, inc=1, device_id={"dev": lax.rem(me + d, n)}, device_id_type=MESH
        )

    each(1, n, greet)

    loads = [
        pltpu.make_async_copy(src, dst, load_sem.at[i])
        for i, (src, dst) in enumerate(
            ((window_hbm, window_ref), (traces_hbm, traces_ref), (dips_hbm, dips_ref))
        )
    ]
    for load in loads:
        load.start()
    edge = jnp.zeros((2 * rp, length), jnp.float32)
    buf[0 : 2 * rp, :] = edge
    buf[(shots + 2) * rp :, :] = edge
    blank = jnp.zeros((TILE, length), jnp.float32)
    for which in range(len(shifts)):
        for row in range(2 * wide + inner):
            line[which, row, 0:TILE, :] = blank
            line[which, row, TILE + shots :, :] = blank
    for load in loads:
        load.wait()

    half = window_ref[0]
    values = traces_ref[0]
    later = lax.broadcasted_iota(jnp.int32, (length, length), 0)
    earlier = lax.broadcasted_iota(jnp.int32, (length, length), 1)
    near = (jnp.abs(later - earlier) <= half).astype(jnp.float32)
    power = jnp.dot(
        values * values, near,
        precision=lax.Precision.HIGHEST, preferred_element_type=jnp.float32,
    )
    sample = lax.broadcasted_iota(jnp.int32, (1, length), 1)
    count = jnp.minimum(sample + half, length - 1) - jnp.maximum(sample - half, 0) + 1
    balanced = values * lax.rsqrt(jnp.maximum(power / count.astype(jnp.float32), FLOOR))
    pad[0:HALF_RECV, :] = jnp.zeros((HALF_RECV, length), jnp.float32)
    pad[HALF_RECV : HALF_RECV + recv, :] = balanced
    tail = pad.shape[0] - HALF_RECV - recv
    pad[HALF_RECV + recv :, :] = jnp.zeros((tail, length), jnp.float32)

    def pack(d):
        send[d] = pad[pl.ds(d * inner, rp), :]

    each(0, n, pack)
    pl.semaphore_wait(barrier, n - 1)

    def block(shot):
        return buf.at[pl.ds(pl.multiple_of((shot + 2) * rp, TILE), rp), :]

    def outgoing(d):
        peer = lax.rem(me + d, n)
        return pltpu.make_async_remote_copy(
            src_ref=send.at[peer],
            dst_ref=block(me),
            send_sem=send_sem.at[d],
            recv_sem=recv_sem.at[d],
            device_id={"dev": peer},
            device_id_type=MESH,
        )

    each(1, n, lambda d: outgoing(d).start())
    for dip in range(-MAXDIP, MAXDIP + 1):
        found = dips_ref[0] == dip
        for i in range(1, dips_ref.shape[0]):
            found = jnp.logical_or(found, dips_ref[i] == dip)
        weight[dip + MAXDIP] = jnp.where(found, 1.0, 0.0).astype(jnp.float32)

    source = lax.broadcasted_iota(jnp.int32, (2 * length, length), 0)
    output = lax.broadcasted_iota(jnp.int32, (2 * length, length), 1)
    in_low = source < length
    at = jnp.where(in_low, source, source - length)
    at = jnp.where(in_low & (at >= 3 * length // 4), at - length, at)
    at = jnp.where(~in_low & (at < length // 4), at + length, at)
    adds = (jnp.abs(at - output) <= HALF_TIME) & (in_low == (output < length // 2))
    band[...] = adds.astype(jnp.float32).astype(jnp.bfloat16)
    buf[pl.ds(pl.multiple_of((me + 2) * rp, TILE), rp), :] = send[me]

    def arrived(d):
        source = lax.rem(me + n - d, n)
        pltpu.make_async_remote_copy(
            src_ref=send.at[source],
            dst_ref=block(source),
            send_sem=send_sem.at[d],
            recv_sem=recv_sem.at[d],
            device_id={"dev": source},
            device_id_type=MESH,
        ).wait_recv()

    each(1, n, arrived)

    lane = lax.broadcasted_iota(jnp.int32, (TILE, length), 1)
    early, late = lane < 3 * length // 4, lane >= length // 4

    def masks(amount):
        if amount > 0:
            wrapped = lane >= length - amount
            return early | wrapped, late & ~wrapped
        wrapped = lane < -amount
        return early & ~wrapped, late | wrapped

    def spread(first):
        here = pl.ds(first + TILE, TILE)
        owns = [buf[pl.ds((first + 2) * rp + r, TILE, stride=rp), :] for r in range(wide)]
        boxes = []
        for total in recv_sums([own * own for own in owns], inner):
            boxes.append(
                [centred_box(jnp.where(keep, total, 0.0)) for keep in (early, late)]
            )
        for which, amount in enumerate(shifts):
            low, high = masks(amount)
            for r, own in enumerate(owns):
                moved = ahead(own, amount)
                line[which, 2 * r, here, :] = jnp.where(low, moved, 0.0)
                line[which, 2 * r + 1, here, :] = jnp.where(high, moved, 0.0)
            target = lane - amount
            target = jnp.where(target < 0, target + length, target)
            target = jnp.where(target >= length, target - length, target)
            for o, (before, after) in enumerate(boxes):
                line[which, 2 * wide + o, here, :] = ahead(
                    jnp.where(target < length // 2, before, after), amount
                )

    def dip_sum(first, row, dip):
        terms = [
            line[shifts.index(k * dip), row, pl.ds(first + TILE + k, TILE), :]
            for k in range(-2, 3)
        ]
        return ((terms[0] + terms[1]) + (terms[3] + terms[4])) + terms[2]

    def scan(first):
        dips = range(-MAXDIP, MAXDIP + 1)
        for i, dip in enumerate(dips):
            for side in range(2):
                squares = []
                for r in range(wide):
                    total = dip_sum(first, 2 * r + side, dip)
                    squares.append(total * total)
                for o, total in enumerate(recv_sums(squares, inner)):
                    row = (i * inner + o) * TILE
                    summed[row : row + TILE, side * length : (side + 1) * length] = total
        value = summed[...]
        numerator = None
        for _ in range(3):
            piece = value.astype(jnp.bfloat16)
            value = value - piece.astype(jnp.float32)
            term = jnp.dot(piece, band[...], preferred_element_type=jnp.float32)
            numerator = term if numerator is None else numerator + term
        for o in range(inner):
            best = None
            for i, dip in enumerate(dips):
                row = (i * inner + o) * TILE
                energy = dip_sum(first, 2 * wide + o, dip)
                current = numerator[row : row + TILE] * weight[i] / (5.0 * energy + 1.0)
                best = current if best is None else jnp.maximum(best, current)
            out_ref[o, pl.ds(first, TILE), :] = best

    energies = spread

    blocks = shots // TILE
    if blocks == 1:
        energies(0)
        scan(0)
    else:
        lax.fori_loop(0, blocks, lambda i, c: (energies(pl.multiple_of(i * TILE, TILE)), c)[1], 0)
        lax.fori_loop(0, blocks, lambda i, c: (scan(pl.multiple_of(i * TILE, TILE)), c)[1], 0)

    each(1, n, lambda d: outgoing(d).wait_send())


def body(n, traces, half_window, dip_slopes):
    _, recv, length = traces.shape
    shots = n
    inner = recv // n
    rp = -(-(inner + 2 * HALF_RECV) // TILE) * TILE
    result = pl.pallas_call(
        functools.partial(kernel, n, shots, recv, inner, rp),
        out_shape=jax.ShapeDtypeStruct((inner, shots, length), jnp.float32),
        in_specs=[
            pl.BlockSpec(memory_space=pltpu.HBM),
            pl.BlockSpec(memory_space=pltpu.HBM),
            pl.BlockSpec(memory_space=pltpu.HBM),
        ],
        out_specs=pl.BlockSpec(memory_space=pltpu.VMEM),
        scratch_shapes=[
            pltpu.VMEM(traces.shape, jnp.float32),
            pltpu.SMEM(half_window.shape, jnp.int32),
            pltpu.SMEM(dip_slopes.shape, jnp.int32),
            pltpu.SemaphoreType.DMA((3,)),
            pltpu.VMEM((recv + rp, length), jnp.float32),
            pltpu.VMEM((n, rp, length), jnp.float32),
            pltpu.VMEM(((shots + 4) * rp, length), jnp.float32),
            pltpu.VMEM((13, 3 * inner + 8, shots + 2 * TILE, length), jnp.float32),
            pltpu.VMEM(((2 * MAXDIP + 1) * inner * TILE, 2 * length), jnp.float32),
            pltpu.VMEM((2 * length, length), jnp.bfloat16),
            pltpu.SMEM((2 * MAXDIP + 1,), jnp.float32),
            pltpu.SemaphoreType.DMA((n,)),
            pltpu.SemaphoreType.DMA((n,)),
        ],
        compiler_params=pltpu.CompilerParams(
            collective_id=0, has_side_effects=True, vmem_limit_bytes=32 * 1024 * 1024
        ),
    )(pltpu.with_memory_space_constraint(traces, pltpu.HBM), half_window, pltpu.with_memory_space_constraint(dip_slopes, pltpu.HBM))
    return jnp.swapaxes(result, 0, 1)


def solution(mesh):
    return jax.shard_map(
        functools.partial(body, mesh.shape["dev"]),
        mesh=mesh,
        in_specs=(P(("grp", "dev"), None, None), P(("grp", "dev")), P()),
        out_specs=P("grp", "dev", None),
        check_vma=False,
    )
```

```python
import functools

import jax
import jax.numpy as jnp
from jax import lax
from jax.experimental import pallas as pl
from jax.experimental.pallas import tpu as pltpu
from jax.sharding import PartitionSpec as P

MESH = pl.DeviceIdType.MESH
FLOOR = 0.05
HALF_RECV = 2
HALF_TIME = 5
MAXDIP = 4
TILE = 8


def ahead(value, amount):
    length = value.shape[-1]
    shift = (length - amount) % length if isinstance(amount, int) else lax.rem(length - amount, length)
    return value if isinstance(amount, int) and amount == 0 else pltpu.roll(value, shift, value.ndim - 1)


def centred_box(value):
    three = (ahead(value, -1) + ahead(value, 1)) + value
    nine = (ahead(three, -3) + ahead(three, 3)) + three
    return nine + (ahead(value, -5) + ahead(value, 5))


def recv_sums(rows, inner):
    if inner == 2:
        common = (rows[1] + rows[2]) + (rows[3] + rows[4])
        return [common + rows[0], common + rows[5]]
    return [functools.reduce(jnp.add, rows[o : o + 5]) for o in range(inner)]


def kernel(
    n, shots, recv, inner, rp,
    traces_hbm, window_ref, dips_hbm, out_ref,
    traces_ref, dips_ref, load_sem,    pad, send, buf, line, summed, band, weight, send_sem, recv_sem,
):
    length = traces_hbm.shape[-1]
    me = lax.axis_index("dev")
    unroll = n <= 16
    wide = inner + 4
    shifts = sorted({k * dip for k in range(3) for dip in range(-MAXDIP, MAXDIP + 1)})

    def each(low, high, body):
        if unroll:
            for i in range(low, high):
                body(i)
        else:
            lax.fori_loop(low, high, lambda i, c: (body(i), c)[1], 0)

    load = pltpu.make_async_copy(traces_hbm, traces_ref, load_sem.at[0])
    load.start()
    load_dips = pltpu.make_async_copy(dips_hbm, dips_ref, load_sem.at[1])
    load_dips.start()
    barrier = pltpu.get_barrier_semaphore()

    def greet(d):
        pl.semaphore_signal(
            barrier, inc=1, device_id={"dev": lax.rem(me + d, n)}, device_id_type=MESH
        )

    each(1, n, greet)

    half = window_ref[0]
    later = lax.broadcasted_iota(jnp.int32, (length, length), 0)
    earlier = lax.broadcasted_iota(jnp.int32, (length, length), 1)
    near = (jnp.abs(later - earlier) <= half).astype(jnp.float32)
    sample = lax.broadcasted_iota(jnp.int32, (1, length), 1)
    count = jnp.minimum(sample + half, length - 1) - jnp.maximum(sample - half, 0) + 1
    pad[0:HALF_RECV, :] = jnp.zeros((HALF_RECV, length), jnp.float32)
    tail = pad.shape[0] - HALF_RECV - recv
    pad[HALF_RECV + recv :, :] = jnp.zeros((tail, length), jnp.float32)
    load.wait()
    values = traces_ref[0]
    power = jnp.dot(
        values * values, near,
        precision=lax.Precision.HIGHEST, preferred_element_type=jnp.float32,
    )
    balanced = values * lax.rsqrt(jnp.maximum(power / count.astype(jnp.float32), FLOOR))
    pad[HALF_RECV : HALF_RECV + recv, :] = balanced

    def pack(d):
        send[d] = pad[pl.ds(d * inner, rp), :]

    each(0, n, pack)
    pl.semaphore_wait(barrier, n - 1)

    def block(shot):
        return buf.at[pl.ds(pl.multiple_of((shot + 2) * rp, TILE), rp), :]

    def outgoing(d):
        peer = lax.rem(me + d, n)
        return pltpu.make_async_remote_copy(
            src_ref=send.at[peer],
            dst_ref=block(me),
            send_sem=send_sem.at[d],
            recv_sem=recv_sem.at[d],
            device_id={"dev": peer},
            device_id_type=MESH,
        )

    each(1, n, lambda d: outgoing(d).start())
    blank = jnp.zeros((TILE, length), jnp.float32)
    for which in range(len(shifts)):
        for row in range(2 * wide + inner):
            line[which, row, 0:TILE, :] = blank
            line[which, row, TILE + shots :, :] = blank

    load_dips.wait()
    for dip in range(-MAXDIP, MAXDIP + 1):
        found = dips_ref[0] == dip
        for i in range(1, dips_ref.shape[0]):
            found = jnp.logical_or(found, dips_ref[i] == dip)
        weight[dip + MAXDIP] = jnp.where(found, 1.0, 0.0).astype(jnp.float32)

    source = lax.broadcasted_iota(jnp.int32, (2 * length, length), 0)
    output = lax.broadcasted_iota(jnp.int32, (2 * length, length), 1)
    in_low = source < length
    at = jnp.where(in_low, source, source - length)
    at = jnp.where(in_low & (at >= 3 * length // 4), at - length, at)
    at = jnp.where(~in_low & (at < length // 4), at + length, at)
    adds = (jnp.abs(at - output) <= HALF_TIME) & (in_low == (output < length // 2))
    band[...] = adds.astype(jnp.float32).astype(jnp.bfloat16)
    buf[pl.ds(pl.multiple_of((me + 2) * rp, TILE), rp), :] = send[me]

    def arrived(d):
        source = lax.rem(me + n - d, n)
        pltpu.make_async_remote_copy(
            src_ref=send.at[source],
            dst_ref=block(source),
            send_sem=send_sem.at[d],
            recv_sem=recv_sem.at[d],
            device_id={"dev": source},
            device_id_type=MESH,
        ).wait_recv()

    each(1, n, arrived)

    lane = lax.broadcasted_iota(jnp.int32, (TILE, length), 1)
    early, late = lane < 3 * length // 4, lane >= length // 4

    def masks(amount):
        if amount > 0:
            wrapped = lane >= length - amount
            return early | wrapped, late & ~wrapped
        wrapped = lane < -amount
        return early & ~wrapped, late | wrapped

    def spread(first):
        here = pl.ds(first + TILE, TILE)
        owns = [buf[pl.ds((first + 2) * rp + r, TILE, stride=rp), :] for r in range(wide)]
        boxes = []
        for total in recv_sums([own * own for own in owns], inner):
            boxes.append(
                [centred_box(jnp.where(keep, total, 0.0)) for keep in (early, late)]
            )
        for which, amount in enumerate(shifts):
            low, high = masks(amount)
            for r, own in enumerate(owns):
                moved = ahead(own, amount)
                line[which, 2 * r, here, :] = jnp.where(low, moved, 0.0)
                line[which, 2 * r + 1, here, :] = jnp.where(high, moved, 0.0)
            target = lane - amount
            target = jnp.where(target < 0, target + length, target)
            target = jnp.where(target >= length, target - length, target)
            for o, (before, after) in enumerate(boxes):
                line[which, 2 * wide + o, here, :] = ahead(
                    jnp.where(target < length // 2, before, after), amount
                )

    def dip_sum(first, row, dip):
        terms = [
            line[shifts.index(k * dip), row, pl.ds(first + TILE + k, TILE), :]
            for k in range(-2, 3)
        ]
        return ((terms[0] + terms[1]) + (terms[3] + terms[4])) + terms[2]

    def scan(first):
        dips = range(-MAXDIP, MAXDIP + 1)
        for i, dip in enumerate(dips):
            for side in range(2):
                squares = []
                for r in range(wide):
                    total = dip_sum(first, 2 * r + side, dip)
                    squares.append(total * total)
                for o, total in enumerate(recv_sums(squares, inner)):
                    row = (i * inner + o) * TILE
                    summed[row : row + TILE, side * length : (side + 1) * length] = total
        value = summed[...]
        numerator = None
        for _ in range(3):
            piece = value.astype(jnp.bfloat16)
            value = value - piece.astype(jnp.float32)
            term = jnp.dot(piece, band[...], preferred_element_type=jnp.float32)
            numerator = term if numerator is None else numerator + term
        for o in range(inner):
            best = None
            for i, dip in enumerate(dips):
                row = (i * inner + o) * TILE
                energy = dip_sum(first, 2 * wide + o, dip)
                current = numerator[row : row + TILE] * weight[i] / (5.0 * energy + 1.0)
                best = current if best is None else jnp.maximum(best, current)
            out_ref[o, pl.ds(first, TILE), :] = best

    energies = spread

    blocks = shots // TILE
    if blocks == 1:
        energies(0)
        scan(0)
    else:
        lax.fori_loop(0, blocks, lambda i, c: (energies(pl.multiple_of(i * TILE, TILE)), c)[1], 0)
        lax.fori_loop(0, blocks, lambda i, c: (scan(pl.multiple_of(i * TILE, TILE)), c)[1], 0)

    each(1, n, lambda d: outgoing(d).wait_send())


def body(n, traces, half_window, dip_slopes):
    _, recv, length = traces.shape
    shots = n
    inner = recv // n
    rp = -(-(inner + 2 * HALF_RECV) // TILE) * TILE
    result = pl.pallas_call(
        functools.partial(kernel, n, shots, recv, inner, rp),
        out_shape=jax.ShapeDtypeStruct((inner, shots, length), jnp.float32),
        in_specs=[
            pl.BlockSpec(memory_space=pltpu.HBM),
            pl.BlockSpec(memory_space=pltpu.SMEM),
            pl.BlockSpec(memory_space=pltpu.HBM),
        ],
        out_specs=pl.BlockSpec(memory_space=pltpu.VMEM),
        scratch_shapes=[
            pltpu.VMEM(traces.shape, jnp.float32),
            pltpu.SMEM(dip_slopes.shape, jnp.int32),
            pltpu.SemaphoreType.DMA((2,)),
            pltpu.VMEM((recv + rp, length), jnp.float32),
            pltpu.VMEM((n, rp, length), jnp.float32),
            pltpu.VMEM(((shots + 4) * rp, length), jnp.float32),
            pltpu.VMEM((13, 3 * inner + 8, shots + 2 * TILE, length), jnp.float32),
            pltpu.VMEM(((2 * MAXDIP + 1) * inner * TILE, 2 * length), jnp.float32),
            pltpu.VMEM((2 * length, length), jnp.bfloat16),
            pltpu.SMEM((2 * MAXDIP + 1,), jnp.float32),
            pltpu.SemaphoreType.DMA((n,)),
            pltpu.SemaphoreType.DMA((n,)),
        ],
        compiler_params=pltpu.CompilerParams(
            collective_id=0, has_side_effects=True, vmem_limit_bytes=32 * 1024 * 1024
        ),
    )(pltpu.with_memory_space_constraint(traces, pltpu.HBM), half_window, pltpu.with_memory_space_constraint(dip_slopes, pltpu.HBM))
    return jnp.swapaxes(result, 0, 1)


def solution(mesh):
    return jax.shard_map(
        functools.partial(body, mesh.shape["dev"]),
        mesh=mesh,
        in_specs=(P(("grp", "dev"), None, None), P(("grp", "dev")), P()),
        out_specs=P("grp", "dev", None),
        check_vma=False,
    )
```
